32 devices in a mesh: dp: 2 (over x), expert: 16 (over z, y, core).
Axes of the slice: x: 2, y: 2, z: 4, core: 2. Of those that a mesh axis runs over, the one named last changes fastest.
Arguments:
- out_grads: bfloat16 [4096, 3584], P(('dp', 'expert')), may hold values from -6 to 6
- route_probs: float32 [4096, 4], P(('dp', 'expert')), may hold values from 0.05 to 1
- expert_ids: int32 [4096, 4], P(('dp', 'expert')), may hold values from 0 to 15, all different within a row; in each aligned block of 128 rows (0 to 127, 128 to 255, ...) at most 48 rows name the same one
- saved_inputs: bfloat16 [4096, 4, 1024], P(('dp', 'expert')), may hold values from -0.59765625 to 0.59765625
- w_latent: bfloat16 [16, 3584, 1024], P('expert'), as said below
- block_exponents: int32 [16, 3584, 8], P('expert'), may hold values from -9 to -6, as said below
Outputs:
- input_grads: bfloat16 [4096, 4, 1024], P(('dp', 'expert'))
- weight_grads: float32 [16, 3584, 1024], P('expert', 'dp')
The draws below stay inside these ranges and needn't reach their ends.
Inputs may be any that keep to these rules, and one draw needn't show every extreme that they name: `expert_ids`: each token names 4 different experts; the 128 tokens of one device name one expert in at most 48 slots, and some expert reaches 48. `block_exponents`: one exponent per 128 consecutive inputs of one output feature. w_latent * 2^(-exponent) lies within 0.45 of a whole number from -9 to 8.
All inputs are finite; a program needn't handle non-finite values.
Results may differ from the reference program's by a relative error of at most 0.012.
Values may be sent and summed in bfloat16 or wider, within the bound.
A program may use at most 128 MiB of HBM per device.

```python
import math
import jax
import jax.numpy as jnp
import numpy as np
from jax import lax

D = 3584
FF = 1024
BLK = 128
TOPK = 4
TOK_DEV = 128
EXPERTS = 16
CAP = 48
TOKENS = 4096
N_DP = 2
N_EXPERT = 16


def weight_parts(key):
    base = jax.random.fold_in(key, 7001)
    exponents = jax.random.randint(jax.random.fold_in(base, 1), (EXPERTS, D, FF // BLK), -9, -5)
    levels = jax.random.randint(jax.random.fold_in(base, 2), (EXPERTS, D, FF), -9, 9)
    return (exponents.astype(jnp.int32), levels, base)


def draw_block_exponents(key, part):
    exponents, levels, base = weight_parts(key)
    return exponents


def draw_w_latent(key, part):
    exponents, levels, base = weight_parts(key)
    offsets = jax.random.uniform(jax.random.fold_in(base, 3), (EXPERTS, D, FF), jnp.float32, -0.3, 0.3)
    shifts = jnp.repeat(-exponents, BLK, axis=2)
    powers = jnp.left_shift(jnp.ones_like(shifts), shifts).astype(jnp.float32)
    return ((levels.astype(jnp.float32) + offsets) / powers).astype(jnp.bfloat16)


def level_of(key, shape, pieces, least, top_value):
    loudness = 1.0
    for dim, parts in pieces:
        steps = jax.random.uniform(jax.random.fold_in(jax.random.fold_in(key, 6), dim), (parts,), jnp.float32, least / len(pieces), top_value / len(pieces))
        loudness = loudness * jnp.repeat(jnp.exp(steps), shape[dim] // parts).reshape((-1,) + (1,) * (len(shape) - 1 - dim))
    return loudness


def routed_block(own_key, own, number, rows, count, top, most, lean):
    sequence = jax.random.permutation(own_key, count)
    crowded, ordinary = shares(count, rows * top, most, lean, True), shares(count, rows * top, most, lean, False)
    places = jnp.arange(count)

    def named(lengths, rotation):
        used = int((lengths > 0).sum())
        fixed = max(1, used // 4)
        moved = fixed + (places - fixed + rotation * (used - fixed)) % max(1, count - fixed)
        return jnp.zeros((count,), jnp.int32).at[sequence[jnp.where(places < fixed, places, moved)]].set(jnp.asarray(lengths, jnp.int32))

    lengths = jnp.where(number % 4 == 0, named(crowded, number // 4), named(ordinary, number - number // 4 - 1))
    mixed = jax.random.permutation(jax.random.fold_in(own, 3), count)
    donor, taker = mixed[0:count // 2 * 2:2], mixed[1:count // 2 * 2:2]
    slack = jnp.minimum(lengths[donor] - 1, most - lengths[taker]) // 2
    slack = jnp.where((donor == sequence[0]) | (taker == sequence[0]) | (lengths[taker] == 0), 0, jnp.maximum(slack, 0))
    moved = jax.random.randint(jax.random.fold_in(own, 4), (count // 2,), 0, 1 << 20) % (slack + 1)
    lengths = lengths.at[donor].add(-moved).at[taker].add(moved)
    members = jnp.searchsorted(jnp.cumsum(lengths), jnp.arange(rows * top), side="right").astype(jnp.int32)
    grid = members.reshape(top, rows).T
    grid = grid[jax.random.permutation(jax.random.fold_in(own, 1), rows)]
    rotation = jax.random.randint(jax.random.fold_in(own, 2), (rows, 1), 0, top)
    return jnp.take_along_axis(grid, (jnp.arange(top)[None, :] + rotation) % top, axis=1)


def shares(amount, total, bound, lean, full):
    portions = [(1 << 20) // math.isqrt(standing ** lean) + 1 for standing in range(1, amount + 1)]
    largest = bound if full else min(bound, max(-(-total // amount), total * portions[0] // sum(portions)))
    least = 1 if total - largest >= amount - 1 else 0
    given, surplus = [largest] + [least] * (amount - 1), total - largest - least * (amount - 1)
    while surplus > 0:
        movable = [i for i in range(1, amount) if given[i] < largest] or [i for i in range(1, amount) if given[i] < bound]
        whole, budget = sum([portions[i] for i in movable]), surplus
        for i in movable:
            addition = min(bound - given[i], max(1, budget * portions[i] // whole), surplus)
            given[i] = given[i] + addition
            surplus = surplus - addition
    return np.array(given)


def normal_values(stream_key, extent, spread, limit, shards=(), kind=jnp.bfloat16):
    factor_of = level_of(stream_key, extent, shards, -0.22, 0.18) if shards else 1.0
    array = jax.random.normal(stream_key, extent, jnp.float32) * spread * factor_of
    return jnp.minimum(jnp.maximum(array, -limit), limit).astype(kind)


def setup_inputs(seed: int = 0) -> dict:
    keys = jax.random.split(jax.random.key(seed), 7)
    out_grads = normal_values(keys[0], (TOKENS, D), 1.0, 6.0, ((0, 32),))
    route_probs = jnp.clip(jnp.exp(math.log(1.0) - 2.9957323 * jax.random.uniform(keys[1], (TOKENS, TOPK), jnp.float32) ** level_of(keys[1], (TOKENS, TOPK), ((0, 32),), -0.2, 0.2)), 0.05, 1.0)
    expert_ids_keys = jax.random.split(jax.random.fold_in(keys[2], 1), TOKENS // TOK_DEV)
    expert_ids_turns = jax.random.permutation(jax.random.fold_in(keys[2], 3), TOKENS // TOK_DEV)
    expert_ids = jax.vmap(lambda own, number: routed_block(jax.random.fold_in(keys[2], 2), own, number, TOK_DEV, EXPERTS, TOPK, CAP, 2))(expert_ids_keys, expert_ids_turns).reshape((TOKENS, TOPK))
    saved_inputs = normal_values(keys[3], (TOKENS, TOPK, FF), 0.1, 0.59765625, ((0, 32),))
    w_latent = draw_w_latent(jax.random.fold_in(keys[6], 71), 0)
    block_exponents = draw_block_exponents(jax.random.fold_in(keys[6], 71), 0)
    return {"out_grads": out_grads, "route_probs": route_probs, "expert_ids": expert_ids, "saved_inputs": saved_inputs, "w_latent": w_latent, "block_exponents": block_exponents}


def dequantize(weight_one, exponent_one):
    shifts = jnp.repeat(-exponent_one, BLK, axis=1)
    powers = jnp.left_shift(jnp.ones_like(shifts), shifts).astype(jnp.float32)
    codes = weight_one.astype(jnp.float32) * powers
    levels = jnp.clip(jnp.floor(codes + 0.5), -8.0, 7.0)
    quantized = (levels / powers).astype(jnp.bfloat16)
    inside = ((codes >= -8.5) & (codes <= 7.5)).astype(jnp.float32)
    return quantized, inside


def reference(out_grads, route_probs, expert_ids, saved_inputs, w_latent, block_exponents):
    slot_total = TOKENS * TOPK
    per_device = TOK_DEV * TOPK
    slot_room = N_EXPERT * CAP
    flat_ids = expert_ids.reshape(-1).astype(jnp.int32)
    grouped = flat_ids.reshape(-1, per_device)
    onehot = (grouped[:, :, None] == jnp.arange(EXPERTS, dtype=jnp.int32)[None, None, :]).astype(jnp.int32)
    before = jnp.cumsum(onehot, axis=1) - onehot
    position = jnp.sum(before * onehot, axis=2).reshape(-1).astype(jnp.int32)
    slot_ids = jnp.arange(slot_total, dtype=jnp.int32)
    device = slot_ids // per_device
    replica = device // N_EXPERT
    source = device % N_EXPERT
    target = (((flat_ids * N_DP + replica) * N_EXPERT + source) * CAP + position).astype(jnp.int32)
    table = jnp.full((EXPERTS * N_DP * slot_room,), slot_total, jnp.int32).at[target].set(slot_ids)
    table = table.reshape(EXPERTS, N_DP, slot_room)
    flat_probs = route_probs.reshape(-1)
    flat_inputs = saved_inputs.reshape(slot_total, FF)

    def one_expert(packed):
        weight_one, exponent_one, rows_all = packed
        quantized, inside = dequantize(weight_one, exponent_one)

        def one_replica(summed, row_ids):
            live = row_ids < slot_total
            safe = jnp.minimum(row_ids, slot_total - 1)
            weights_here = jnp.where(live, flat_probs[safe], jnp.zeros((), jnp.float32))
            grads = (weights_here[:, None] * out_grads[safe // TOPK].astype(jnp.float32)).astype(jnp.bfloat16)
            inputs_here = jnp.where(live[:, None], flat_inputs[safe], jnp.zeros((), jnp.bfloat16))
            back = jnp.dot(grads, quantized, preferred_element_type=jnp.float32).astype(jnp.bfloat16)
            partial_sum = lax.dot_general(grads, inputs_here, (((0,), (0,)), ((), ())), preferred_element_type=jnp.float32)
            rounded = lax.optimization_barrier(partial_sum.astype(jnp.bfloat16)).astype(jnp.float32)
            return summed + rounded, back

        summed, backs = lax.scan(one_replica, jnp.zeros((D, FF), jnp.float32), rows_all)
        return inside * summed, backs

    weight_grads, backs = lax.map(one_expert, (w_latent, block_exponents, table))
    input_grads = jnp.zeros((slot_total + 1, FF), jnp.bfloat16).at[table.reshape(-1)].set(backs.reshape(-1, FF))
    input_grads = input_grads[:slot_total].reshape(TOKENS, TOPK, FF)
    return input_grads, weight_grads
```

```python
import functools

import jax
import jax.numpy as jnp
from jax import lax
from jax.experimental import pallas as pl
from jax.experimental.pallas import tpu as pltpu
from jax.sharding import PartitionSpec as P

BLK = 128
PLANE = 4
PIECES = 2
VMEM_LIMIT = 56 * 1024 * 1024


def pack_kernel(n, capp, ids_ref, probs_ref, saved_ref, send_ref, meta_ref):
    slots = ids_ref.shape[1]
    ids = ids_ref[...]
    expert_rows = lax.broadcasted_iota(jnp.int32, (n, slots), 0)
    onehot = (expert_rows == ids).astype(jnp.float32)
    earlier = lax.broadcasted_iota(jnp.int32, (slots, slots), 0)
    later = lax.broadcasted_iota(jnp.int32, (slots, slots), 1)
    before = jnp.dot(
        onehot.astype(jnp.bfloat16),
        (earlier < later).astype(jnp.float32).astype(jnp.bfloat16),
        preferred_element_type=jnp.float32,
    )
    position = jnp.sum(before * onehot, axis=0, keepdims=True)
    target = ids.astype(jnp.float32) * float(capp) + position
    meta_ref[...] = jnp.zeros_like(meta_ref)
    meta_ref[0:1, :] = target
    meta_ref[1:2, :] = probs_ref[...]
    target = target.astype(jnp.int32)
    places = lax.broadcasted_iota(jnp.int32, (capp, slots), 0)

    @pl.loop(0, n)
    def _(e):
        pick = (places + e * capp == target).astype(jnp.float32).astype(jnp.bfloat16)
        send_ref[e] = jnp.dot(pick, saved_ref[...], preferred_element_type=jnp.float32).astype(
            jnp.bfloat16
        )


def exchange_kernel(
    n, own, xs, meta, g, x, m, local_sem, up_sem, down_sem, y_sem, core_sem, x_send, x_recv, m_send, m_recv, g_recv
):
    me = lax.axis_index("expert")
    depth = n // PLANE
    z = me // PLANE
    lane = lax.rem(me, PLANE)
    core_lane = lane + 1 - 2 * lax.rem(lane, 2)
    y_lane = lax.rem(lane + 2, PLANE)
    core_mate = z * PLANE + core_lane
    y_mate = z * PLANE + y_lane
    rows = own.shape[0] // PIECES

    barrier = pltpu.get_barrier_semaphore()
    for d in range(1, n):
        pl.semaphore_signal(barrier, inc=1, device_id={"expert": lax.rem(me + d, n)})
    pl.semaphore_wait(barrier, n - 1)

    def cp(block, k, dest, send, from_own=False):
        part = pl.ds(k * rows, rows)
        return pltpu.make_async_remote_copy(
            src_ref=own.at[part] if from_own else g.at[block, part],
            dst_ref=g.at[block, part],
            send_sem=send,
            recv_sem=g_recv.at[block, k],
            device_id={"expert": dest},
        )

    def got(block, k):
        cp(block, k, me, up_sem.at[0, k]).wait_recv()

    def hand_on(bz, k, up, down, from_own=False):
        block = bz * PLANE + lane
        if up:
            @pl.when(z + 1 < depth)
            def _():
                cp(block, k, me + PLANE, up_sem.at[bz, k], from_own).start()
        if down:
            @pl.when(z >= 1)
            def _():
                cp(block, k, me - PLANE, down_sem.at[bz, k], from_own).start()
        cp(block, k, y_mate, y_sem.at[bz, k], from_own).start()
        cp(block, k, core_mate, core_sem.at[bz, k], from_own).start()

    for k in range(PIECES):
        hand_on(z, k, True, True, from_own=True)

    locals_ = [
        pltpu.make_async_copy(own, g.at[me], local_sem.at[0]),
        pltpu.make_async_copy(xs.at[me], x.at[me], local_sem.at[1]),
        pltpu.make_async_copy(meta, m.at[me], local_sem.at[2]),
    ]
    for c in locals_:
        c.start()

    def xcp(d):
        dest = lax.rem(me + d, n)
        return pltpu.make_async_remote_copy(
            src_ref=xs.at[dest], dst_ref=x.at[me], send_sem=x_send.at[d], recv_sem=x_recv.at[me],
            device_id={"expert": dest},
        )

    def mcp(d):
        return pltpu.make_async_remote_copy(
            src_ref=meta, dst_ref=m.at[me], send_sem=m_send.at[d], recv_sem=m_recv.at[me],
            device_id={"expert": lax.rem(me + d, n)},
        )

    for d in range(1, n):
        mcp(d).start()
        xcp(d).start()

    def relay(bz, k):
        block = bz * PLANE + y_lane
        got(block, k)
        cp(block, k, core_mate, core_sem.at[depth + bz, k]).start()

    for step in range(1, depth + 1):
        for k in range(PIECES):
            if step < depth:
                @pl.when(z - step >= 0)
                def _():
                    got((z - step) * PLANE + lane, k)
                    hand_on(z - step, k, True, False)

                @pl.when(z + step < depth)
                def _():
                    got((z + step) * PLANE + lane, k)
                    hand_on(z + step, k, False, True)
            last = step - 1
            @pl.when(z - last >= 0)
            def _():
                relay(z - last, k)

            if last:
                @pl.when(z + last < depth)
                def _():
                    relay(z + last, k)

    for bz in range(depth):
        for k in range(PIECES):
            got(bz * PLANE + core_lane, k)
            got(bz * PLANE + lax.rem(core_lane + 2, PLANE), k)
    for d in range(1, n):
        peer = lax.rem(me + d, n)
        pltpu.make_async_remote_copy(
            src_ref=xs.at[peer], dst_ref=x.at[peer], send_sem=x_send.at[d], recv_sem=x_recv.at[peer],
            device_id={"expert": peer},
        ).wait_recv()
        pltpu.make_async_remote_copy(
            src_ref=meta, dst_ref=m.at[peer], send_sem=m_send.at[d], recv_sem=m_recv.at[peer],
            device_id={"expert": peer},
        ).wait_recv()
    for d in range(1, n):
        xcp(d).wait_send()
        mcp(d).wait_send()
    for bz in range(depth):
        for k in range(PIECES):
            block = bz * PLANE + lane

            @pl.when((z + 1 < depth) & (bz <= z))
            def _():
                cp(block, k, me, up_sem.at[bz, k]).wait_send()

            @pl.when((z >= 1) & (bz >= z))
            def _():
                cp(block, k, me, down_sem.at[bz, k]).wait_send()

            cp(block, k, y_mate, y_sem.at[bz, k]).wait_send()
            cp(block, k, core_mate, core_sem.at[bz, k]).wait_send()
            cp(block, k, core_mate, core_sem.at[depth + bz, k]).wait_send()
    for c in locals_:
        c.wait()


def powers_of(exponents):
    one = jnp.ones_like(exponents)
    up = jnp.left_shift(one, -exponents).astype(jnp.float32)
    down = jnp.left_shift(one, exponents + 16).astype(jnp.float32) * (2.0**-16)
    return up, down


def expert_kernel(n, capp, top, me_ref, m_ref, g_ref, x_ref, w_ref, e_ref, back_ref, part_ref, sel, prob, sg, wq, acc):
    step = pl.program_id(0)
    tok = g_ref.shape[0] // n
    slots = m_ref.shape[2]

    @pl.when(step == 0)
    def _():
        acc[...] = jnp.zeros_like(acc)
        places = lax.broadcasted_iota(jnp.int32, (capp, slots), 0) + me_ref[0] * capp
        token_of = lax.broadcasted_iota(jnp.int32, (slots, tok), 0)
        first = lax.broadcasted_iota(jnp.int32, (slots, tok), 1) * top
        owner = ((token_of >= first) & (token_of < first + top)).astype(jnp.float32).astype(jnp.bfloat16)

        @pl.loop(0, n)
        def _(s):
            here = (places == m_ref[s, 0:1, :].astype(jnp.int32)).astype(jnp.float32)
            sel[s] = jnp.dot(
                here.astype(jnp.bfloat16), owner, preferred_element_type=jnp.float32
            ).astype(jnp.bfloat16)
            weight = jnp.sum(here * m_ref[s, 1:2, :], axis=1, keepdims=True)
            prob[s] = jnp.broadcast_to(weight, prob.shape[1:])

    for s in range(n):
        picked = jnp.dot(sel[s], g_ref[s * tok : (s + 1) * tok, :], preferred_element_type=jnp.float32)
        sg[s * capp : (s + 1) * capp, :] = (picked * prob[s][:, 0:1]).astype(jnp.bfloat16)
    up, down = powers_of(e_ref[...])
    for j in range(e_ref.shape[1]):
        cols = slice(j * BLK, (j + 1) * BLK)
        codes = w_ref[:, cols].astype(jnp.float32) * up[:, j : j + 1]
        levels = jnp.clip(jnp.floor(codes + 0.5), -8.0, 7.0)
        wq[:, cols] = (levels * down[:, j : j + 1]).astype(jnp.bfloat16)
    acc[...] += jnp.dot(sg[...], wq[...], preferred_element_type=jnp.float32)
    part_ref[...] = lax.dot_general(
        sg[...], x_ref[...], (((0,), (0,)), ((), ())), preferred_element_type=jnp.float32
    ).astype(jnp.bfloat16)

    @pl.when(step == pl.num_programs(0) - 1)
    def _():
        back_ref[...] = acc[...].astype(jnp.bfloat16)


def keep_kernel(at_ref, s_ref, w_ref, e_ref, o_ref):
    up, _ = powers_of(e_ref[...])
    for j in range(e_ref.shape[1]):
        cols = slice(j * BLK, (j + 1) * BLK)
        codes = w_ref[:, cols].astype(jnp.float32) * up[:, j : j + 1]
        inside = ((codes >= -8.5) & (codes <= 7.5)).astype(jnp.float32)
        o_ref[:, cols] = s_ref[:, cols].astype(jnp.float32) * inside


def tile_of(size, most):
    return max(t for t in range(16, most + 1, 16) if size % t == 0)


def local(out_grads, route_probs, expert_ids, saved_inputs, w_latent, block_exponents):
    n = lax.axis_size("expert")
    tok, top = expert_ids.shape
    width = out_grads.shape[1]
    hidden = saved_inputs.shape[2]
    slots = tok * top
    capacity = tok * top * 3 // (2 * n)
    capp = -(-capacity // 16) * 16
    blocks = block_exponents.shape[2]
    bf16, f32 = jnp.bfloat16, jnp.float32
    vmem = pl.BlockSpec(memory_space=pltpu.VMEM)
    anyspace = pl.BlockSpec(memory_space=pl.ANY)
    params = functools.partial(pltpu.CompilerParams, vmem_limit_bytes=VMEM_LIMIT)

    sends, meta = pl.pallas_call(
        functools.partial(pack_kernel, n, capp),
        out_shape=(
            jax.ShapeDtypeStruct((n, capp, hidden), bf16),
            jax.ShapeDtypeStruct((8, slots), f32),
        ),
        in_specs=[vmem] * 3,
        out_specs=(vmem, vmem),
        compiler_params=params(),
        name="pack_slots",
    )(expert_ids.reshape(1, slots), route_probs.reshape(1, slots), saved_inputs.reshape(slots, hidden))

    depth = n // PLANE
    dma = pltpu.SemaphoreType.DMA
    g, x, m = pl.pallas_call(
        functools.partial(exchange_kernel, n),
        out_shape=(
            jax.ShapeDtypeStruct((n, tok, width), bf16),
            jax.ShapeDtypeStruct((n, capp, hidden), bf16),
            jax.ShapeDtypeStruct((n, 8, slots), f32),
        ),
        in_specs=[anyspace] * 3,
        out_specs=(anyspace,) * 3,
        scratch_shapes=[
            dma((3,)),
            dma((depth, PIECES)),
            dma((depth, PIECES)),
            dma((depth, PIECES)),
            dma((2 * depth, PIECES)),
            dma((n,)),
            dma((n,)),
            dma((n,)),
            dma((n,)),
            dma((n, PIECES)),
        ],
        compiler_params=pltpu.CompilerParams(collective_id=0, has_side_effects=True),
        name="exchange",
    )(out_grads, sends, meta)

    me = lax.axis_index("expert").astype(jnp.int32).reshape(1)
    chunk = 512
    back, partial = pl.pallas_call(
        functools.partial(expert_kernel, n, capp, top),
        grid=(width // chunk,),
        out_shape=(
            jax.ShapeDtypeStruct((n * capp, hidden), bf16),
            jax.ShapeDtypeStruct((width, hidden), bf16),
        ),
        in_specs=[
            pl.BlockSpec(memory_space=pltpu.SMEM),
            pl.BlockSpec((n, 8, slots), lambda i: (0, 0, 0)),
            pl.BlockSpec((n * tok, chunk), lambda i: (0, i)),
            pl.BlockSpec((n * capp, hidden), lambda i: (0, 0)),
            pl.BlockSpec((chunk, hidden), lambda i: (i, 0)),
            pl.BlockSpec((chunk, blocks), lambda i: (i, 0)),
        ],
        out_specs=(
            pl.BlockSpec((n * capp, hidden), lambda i: (0, 0)),
            pl.BlockSpec((chunk, hidden), lambda i: (i, 0)),
        ),
        scratch_shapes=[
            pltpu.VMEM((n, capp, tok), bf16),
            pltpu.VMEM((n, capp, 128), f32),
            pltpu.VMEM((n * capp, chunk), bf16),
            pltpu.VMEM((chunk, hidden), bf16),
            pltpu.VMEM((n * capp, hidden), f32),
        ],
        compiler_params=params(),
        name="expert",
    )(me, m, g.reshape(n * tok, width), x.reshape(n * capp, hidden), w_latent[0], block_exponents[0])

    returned = lax.all_to_all(
        back.reshape(n, capp, hidden), "expert", split_axis=0, concat_axis=0, tiled=True
    )
    target = meta[0].astype(jnp.int32)
    input_grads = returned.reshape(n * capp, hidden)[target].reshape(tok, top, hidden)

    summed = lax.psum_scatter(partial, "dp", scatter_dimension=0, tiled=True)
    share = summed.shape[0]
    tile = tile_of(share, 256)
    tiles = share // tile
    at = (lax.axis_index("dp") * tiles).astype(jnp.int32).reshape(1)
    weight_grads = pl.pallas_call(
        keep_kernel,
        grid_spec=pltpu.PrefetchScalarGridSpec(
            num_scalar_prefetch=1,
            grid=(tiles,),
            in_specs=[
                pl.BlockSpec((tile, hidden), lambda i, at: (i, 0)),
                pl.BlockSpec((tile, hidden), lambda i, at: (at[0] + i, 0)),
                pl.BlockSpec((tile, blocks), lambda i, at: (at[0] + i, 0)),
            ],
            out_specs=pl.BlockSpec((tile, hidden), lambda i, at: (i, 0)),
        ),
        out_shape=jax.ShapeDtypeStruct((share, hidden), f32),
        compiler_params=params(),
        name="keep",
    )(at, summed, w_latent[0], block_exponents[0])
    return (input_grads, weight_grads[None])


def solution(mesh):
    placed = (
        P(("dp", "expert"), None),
        P(("dp", "expert"), None),
        P(("dp", "expert"), None),
        P(("dp", "expert"), None, None),
        P("expert", None, None),
        P("expert", None, None),
    )
    return jax.shard_map(
        local,
        mesh=mesh,
        in_specs=placed,
        out_specs=(P(("dp", "expert"), None, None), P("expert", "dp", None)),
        check_vma=False,
    )
```

```python
import functools

import jax
import jax.numpy as jnp
from jax import lax
from jax.experimental import pallas as pl
from jax.experimental.pallas import tpu as pltpu
from jax.sharding import PartitionSpec as P

BLK = 128
PLANE = 4
PIECES = 2
VMEM_LIMIT = 56 * 1024 * 1024
SHARE_TILE = 256


def pack_kernel(n, capp, ids_ref, probs_ref, saved_ref, send_ref, meta_ref):
    slots = ids_ref.shape[1]
    ids = ids_ref[...]
    expert_rows = lax.broadcasted_iota(jnp.int32, (n, slots), 0)
    onehot = (expert_rows == ids).astype(jnp.float32)
    earlier = lax.broadcasted_iota(jnp.int32, (slots, slots), 0)
    later = lax.broadcasted_iota(jnp.int32, (slots, slots), 1)
    before = jnp.dot(
        onehot.astype(jnp.bfloat16),
        (earlier < later).astype(jnp.float32).astype(jnp.bfloat16),
        preferred_element_type=jnp.float32,
    )
    position = jnp.sum(before * onehot, axis=0, keepdims=True)
    target = ids.astype(jnp.float32) * float(capp) + position
    meta_ref[...] = jnp.zeros_like(meta_ref)
    meta_ref[0:1, :] = target
    meta_ref[1:2, :] = probs_ref[...]
    target = target.astype(jnp.int32)
    places = lax.broadcasted_iota(jnp.int32, (capp, slots), 0)

    @pl.loop(0, n)
    def _(e):
        pick = (places + e * capp == target).astype(jnp.float32).astype(jnp.bfloat16)
        send_ref[e] = jnp.dot(pick, saved_ref[...], preferred_element_type=jnp.float32).astype(
            jnp.bfloat16
        )


def exchange_kernel(
    n, own, xs, meta, g, x, m, local_sem, up_sem, down_sem, y_sem, core_sem, x_send, x_recv, m_send, m_recv, g_recv
):
    me = lax.axis_index("expert")
    depth = n // PLANE
    z = me // PLANE
    lane = lax.rem(me, PLANE)
    core_lane = lane + 1 - 2 * lax.rem(lane, 2)
    y_lane = lax.rem(lane + 2, PLANE)
    core_mate = z * PLANE + core_lane
    y_mate = z * PLANE + y_lane
    rows = own.shape[0] // PIECES

    barrier = pltpu.get_barrier_semaphore()
    for d in range(1, n):
        pl.semaphore_signal(barrier, inc=1, device_id={"expert": lax.rem(me + d, n)})
    pl.semaphore_wait(barrier, n - 1)

    def cp(block, k, dest, send, from_own=False):
        part = pl.ds(k * rows, rows)
        return pltpu.make_async_remote_copy(
            src_ref=own.at[part] if from_own else g.at[block, part],
            dst_ref=g.at[block, part],
            send_sem=send,
            recv_sem=g_recv.at[block, k],
            device_id={"expert": dest},
        )

    def got(block, k):
        cp(block, k, me, up_sem.at[0, k]).wait_recv()

    def hand_on(bz, k, up, down, from_own=False):
        block = bz * PLANE + lane
        if up:
            @pl.when(z + 1 < depth)
            def _():
                cp(block, k, me + PLANE, up_sem.at[bz, k], from_own).start()
        if down:
            @pl.when(z >= 1)
            def _():
                cp(block, k, me - PLANE, down_sem.at[bz, k], from_own).start()
        cp(block, k, y_mate, y_sem.at[bz, k], from_own).start()
        cp(block, k, core_mate, core_sem.at[bz, k], from_own).start()

    for k in range(PIECES):
        hand_on(z, k, True, True, from_own=True)

    locals_ = [
        pltpu.make_async_copy(own, g.at[me], local_sem.at[0]),
        pltpu.make_async_copy(xs.at[me], x.at[me], local_sem.at[1]),
        pltpu.make_async_copy(meta, m.at[me], local_sem.at[2]),
    ]
    for c in locals_:
        c.start()

    def xcp(d):
        dest = lax.rem(me + d, n)
        return pltpu.make_async_remote_copy(
            src_ref=xs.at[dest], dst_ref=x.at[me], send_sem=x_send.at[d], recv_sem=x_recv.at[me],
            device_id={"expert": dest},
        )

    def mcp(d):
        return pltpu.make_async_remote_copy(
            src_ref=meta, dst_ref=m.at[me], send_sem=m_send.at[d], recv_sem=m_recv.at[me],
            device_id={"expert": lax.rem(me + d, n)},
        )

    for d in range(1, n):
        mcp(d).start()
        xcp(d).start()

    def relay(bz, k):
        block = bz * PLANE + y_lane
        got(block, k)
        cp(block, k, core_mate, core_sem.at[depth + bz, k]).start()

    for step in range(1, depth + 1):
        for k in range(PIECES):
            if step < depth:
                @pl.when(z - step >= 0)
                def _():
                    got((z - step) * PLANE + lane, k)
                    hand_on(z - step, k, True, False)

                @pl.when(z + step < depth)
                def _():
                    got((z + step) * PLANE + lane, k)
                    hand_on(z + step, k, False, True)
            last = step - 1
            @pl.when(z - last >= 0)
            def _():
                relay(z - last, k)

            if last:
                @pl.when(z + last < depth)
                def _():
                    relay(z + last, k)

    for bz in range(depth):
        for k in range(PIECES):
            got(bz * PLANE + core_lane, k)
            got(bz * PLANE + lax.rem(core_lane + 2, PLANE), k)
    for d in range(1, n):
        peer = lax.rem(me + d, n)
        pltpu.make_async_remote_copy(
            src_ref=xs.at[peer], dst_ref=x.at[peer], send_sem=x_send.at[d], recv_sem=x_recv.at[peer],
            device_id={"expert": peer},
        ).wait_recv()
        pltpu.make_async_remote_copy(
            src_ref=meta, dst_ref=m.at[peer], send_sem=m_send.at[d], recv_sem=m_recv.at[peer],
            device_id={"expert": peer},
        ).wait_recv()
    for d in range(1, n):
        xcp(d).wait_send()
        mcp(d).wait_send()
    for bz in range(depth):
        for k in range(PIECES):
            block = bz * PLANE + lane

            @pl.when((z + 1 < depth) & (bz <= z))
            def _():
                cp(block, k, me, up_sem.at[bz, k]).wait_send()

            @pl.when((z >= 1) & (bz >= z))
            def _():
                cp(block, k, me, down_sem.at[bz, k]).wait_send()

            cp(block, k, y_mate, y_sem.at[bz, k]).wait_send()
            cp(block, k, core_mate, core_sem.at[bz, k]).wait_send()
            cp(block, k, core_mate, core_sem.at[depth + bz, k]).wait_send()
    for c in locals_:
        c.wait()


def gather_kernel(
    dp, n, own, xs, meta, g, x, m, local_sem, a_send, up_sem, down_sem, y_sem, core_sem,
    x_send, x_recv, m_send, m_recv, g_recv, fx_send, fm_send
):
    me = lax.axis_index("expert")
    r = lax.axis_index("dp")
    depth = n // PLANE
    z = me // PLANE
    lane = lax.rem(me, PLANE)
    core_lane = lane + 1 - 2 * lax.rem(lane, 2)
    y_lane = lax.rem(lane + 2, PLANE)
    core_mate = z * PLANE + core_lane
    y_mate = z * PLANE + y_lane
    reps = [lax.rem(r + k, dp) for k in range(dp)]

    barrier = pltpu.get_barrier_semaphore()
    for d in range(1, n):
        pl.semaphore_signal(barrier, inc=1, device_id={"expert": lax.rem(me + d, n)})
    for k in range(1, dp):
        pl.semaphore_signal(barrier, inc=1, device_id={"dp": reps[k]})
    pl.semaphore_wait(barrier, n - 1 + dp - 1)

    def across(k):
        return pltpu.make_async_remote_copy(
            src_ref=own.at[reps[k]], dst_ref=g.at[r, me], send_sem=a_send.at[k], recv_sem=g_recv.at[r, me],
            device_id={"dp": reps[k]},
        )

    def cp(block, k, dest, send, from_own=False):
        return pltpu.make_async_remote_copy(
            src_ref=own.at[r] if from_own else g.at[reps[k], block],
            dst_ref=g.at[reps[k], block],
            send_sem=send,
            recv_sem=g_recv.at[reps[k], block],
            device_id={"expert": dest},
        )

    def got(block, k):
        cp(block, k, me, up_sem.at[0, k]).wait_recv()

    def hand_on(bz, k, up, down, from_own=False):
        block = bz * PLANE + lane
        if up:
            @pl.when(z + 1 < depth)
            def _():
                cp(block, k, me + PLANE, up_sem.at[bz, k], from_own).start()
        if down:
            @pl.when(z >= 1)
            def _():
                cp(block, k, me - PLANE, down_sem.at[bz, k], from_own).start()
        cp(block, k, y_mate, y_sem.at[bz, k], from_own).start()
        cp(block, k, core_mate, core_sem.at[bz, k], from_own).start()

    for k in range(1, dp):
        across(k).start()
    hand_on(z, 0, True, True, from_own=True)

    locals_ = [
        pltpu.make_async_copy(own.at[r], g.at[r, me], local_sem.at[0]),
        pltpu.make_async_copy(xs.at[me], x.at[r, me], local_sem.at[1]),
        pltpu.make_async_copy(meta, m.at[r, me], local_sem.at[2]),
    ]
    for c in locals_:
        c.start()

    def xcp(d):
        dest = lax.rem(me + d, n)
        return pltpu.make_async_remote_copy(
            src_ref=xs.at[dest], dst_ref=x.at[r, me], send_sem=x_send.at[d], recv_sem=x_recv.at[r, me],
            device_id={"expert": dest},
        )

    def mcp(d):
        return pltpu.make_async_remote_copy(
            src_ref=meta, dst_ref=m.at[r, me], send_sem=m_send.at[d], recv_sem=m_recv.at[r, me],
            device_id={"expert": lax.rem(me + d, n)},
        )

    for d in range(1, n):
        mcp(d).start()
        xcp(d).start()

    def forward(s, k, own_block=False):
        return (
            pltpu.make_async_remote_copy(
                src_ref=xs.at[s] if own_block else x.at[r, s], dst_ref=x.at[r, s],
                send_sem=fx_send.at[k, s], recv_sem=x_recv.at[r, s], device_id={"dp": reps[k]},
            ),
            pltpu.make_async_remote_copy(
                src_ref=meta if own_block else m.at[r, s], dst_ref=m.at[r, s],
                send_sem=fm_send.at[k, s], recv_sem=m_recv.at[r, s], device_id={"dp": reps[k]},
            ),
        )

    def arrived(rep, s):
        pltpu.make_async_remote_copy(
            src_ref=x.at[rep, s], dst_ref=x.at[rep, s], send_sem=x_send.at[0], recv_sem=x_recv.at[rep, s],
            device_id={"dp": r},
        ).wait_recv()
        pltpu.make_async_remote_copy(
            src_ref=m.at[rep, s], dst_ref=m.at[rep, s], send_sem=m_send.at[0], recv_sem=m_recv.at[rep, s],
            device_id={"dp": r},
        ).wait_recv()

    def slots_of_plane(pz):
        for i in range(PLANE):
            arrived(r, pz * PLANE + i)
            for k in range(1, dp):
                for c in forward(pz * PLANE + i, k):
                    c.start()

    for k in range(1, dp):
        for c in forward(me, k, True):
            c.start()
        got(me, k)
        hand_on(z, k, True, True)

    def relay(bz, k):
        block = bz * PLANE + y_lane
        got(block, k)
        cp(block, k, core_mate, core_sem.at[depth + bz, k]).start()

    for step in range(1, depth + 1):
        last = step - 1
        for k in range(dp):
            if step < depth:
                @pl.when(z - step >= 0)
                def _():
                    got((z - step) * PLANE + lane, k)
                    hand_on(z - step, k, True, False)

                @pl.when(z + step < depth)
                def _():
                    got((z + step) * PLANE + lane, k)
                    hand_on(z + step, k, False, True)
            @pl.when(z - last >= 0)
            def _():
                relay(z - last, k)

            if last:
                @pl.when(z + last < depth)
                def _():
                    relay(z + last, k)
        if last == 0:
            for i in range(1, PLANE):
                s = z * PLANE + lax.rem(lane + i, PLANE)
                arrived(r, s)
                for k in range(1, dp):
                    for c in forward(s, k):
                        c.start()
        else:
            @pl.when(z - last >= 0)
            def _():
                slots_of_plane(z - last)

            @pl.when(z + last < depth)
            def _():
                slots_of_plane(z + last)

    for bz in range(depth):
        for k in range(dp):
            got(bz * PLANE + core_lane, k)
            got(bz * PLANE + lax.rem(core_lane + 2, PLANE), k)
    for k in range(1, dp):
        for s in range(n):
            arrived(reps[k], s)
    for d in range(1, n):
        xcp(d).wait_send()
        mcp(d).wait_send()
    for k in range(1, dp):
        across(k).wait_send()
        for s in range(n):
            for c in forward(s, k):
                c.wait_send()
    for bz in range(depth):
        for k in range(dp):
            block = bz * PLANE + lane

            @pl.when((z + 1 < depth) & (bz <= z))
            def _():
                cp(block, k, me, up_sem.at[bz, k]).wait_send()

            @pl.when((z >= 1) & (bz >= z))
            def _():
                cp(block, k, me, down_sem.at[bz, k]).wait_send()

            cp(block, k, y_mate, y_sem.at[bz, k]).wait_send()
            cp(block, k, core_mate, core_sem.at[bz, k]).wait_send()
            cp(block, k, core_mate, core_sem.at[depth + bz, k]).wait_send()
    for c in locals_:
        c.wait()


def return_kernel(dp, n, part, ret, inbox, total, a_send, a_recv, local_sem, send, recv):
    me = lax.axis_index("expert")
    r = lax.axis_index("dp")
    depth = n // PLANE
    z = me // PLANE
    lane = lax.rem(me, PLANE)
    reps = [lax.rem(r + k, dp) for k in range(dp)]
    planes = [lax.rem(z + 1 + i, depth) * PLANE for i in range(depth)]

    barrier = pltpu.get_barrier_semaphore()
    for d in range(1, n):
        pl.semaphore_signal(barrier, inc=1, device_id={"expert": lax.rem(me + d, n)})
    for k in range(1, dp):
        pl.semaphore_signal(barrier, inc=1, device_id={"dp": reps[k]})
    pl.semaphore_wait(barrier, n - 1 + dp - 1)

    def across(i, k):
        return pltpu.make_async_remote_copy(
            src_ref=part.at[reps[k], pl.ds(planes[i], PLANE)],
            dst_ref=inbox.at[dp - k - 1, pl.ds(planes[i], PLANE)],
            send_sem=a_send.at[k - 1, i],
            recv_sem=a_recv.at[dp - k - 1, i],
            device_id={"dp": reps[k]},
        )

    def back(dest):
        return pltpu.make_async_remote_copy(
            src_ref=total.at[dest], dst_ref=ret.at[me], send_sem=send.at[dest], recv_sem=recv.at[me],
            device_id={"expert": dest},
        )

    for i in range(depth):
        for k in range(1, dp):
            across(i, k).start()
    for i in range(depth):
        for k in range(1, dp):
            across(i, k).wait_recv()
        for j in range(PLANE):
            row = planes[i] + j
            value = part[r, row].astype(jnp.float32)
            for k in range(1, dp):
                value = value + inbox[k - 1, row].astype(jnp.float32)
            total[row] = value.astype(jnp.bfloat16)
        for j in range(PLANE):
            if i < depth - 1:
                back(planes[i] + j).start()
            elif j:
                back(z * PLANE + lax.rem(lane + j, PLANE)).start()
    mine = pltpu.make_async_copy(total.at[me], ret.at[me], local_sem.at[0])
    mine.start()
    for d in range(1, n):
        peer = lax.rem(me + d, n)
        pltpu.make_async_remote_copy(
            src_ref=total.at[peer], dst_ref=ret.at[peer], send_sem=send.at[peer], recv_sem=recv.at[peer],
            device_id={"expert": peer},
        ).wait_recv()
    for d in range(1, n):
        back(lax.rem(me + d, n)).wait_send()
    for i in range(depth):
        for k in range(1, dp):
            across(i, k).wait_send()
    mine.wait()


def powers_of(exponents):
    one = jnp.ones_like(exponents)
    up = jnp.left_shift(one, -exponents).astype(jnp.float32)
    down = jnp.left_shift(one, exponents + 16).astype(jnp.float32) * (2.0**-16)
    return up, down


def expert_kernel(n, capp, top, me_ref, m_ref, g_ref, x_ref, w_ref, e_ref, back_ref, part_ref, sel, prob, sg, wq, acc):
    step = pl.program_id(0)
    tok = g_ref.shape[0] // n
    slots = m_ref.shape[2]

    @pl.when(step == 0)
    def _():
        acc[...] = jnp.zeros_like(acc)
        places = lax.broadcasted_iota(jnp.int32, (capp, slots), 0) + me_ref[0] * capp
        token_of = lax.broadcasted_iota(jnp.int32, (slots, tok), 0)
        first = lax.broadcasted_iota(jnp.int32, (slots, tok), 1) * top
        owner = ((token_of >= first) & (token_of < first + top)).astype(jnp.float32).astype(jnp.bfloat16)

        @pl.loop(0, n)
        def _(s):
            here = (places == m_ref[s, 0:1, :].astype(jnp.int32)).astype(jnp.float32)
            sel[s] = jnp.dot(
                here.astype(jnp.bfloat16), owner, preferred_element_type=jnp.float32
            ).astype(jnp.bfloat16)
            weight = jnp.sum(here * m_ref[s, 1:2, :], axis=1, keepdims=True)
            prob[s] = jnp.broadcast_to(weight, prob.shape[1:])

    for s in range(n):
        picked = jnp.dot(sel[s], g_ref[s * tok : (s + 1) * tok, :], preferred_element_type=jnp.float32)
        sg[s * capp : (s + 1) * capp, :] = (picked * prob[s][:, 0:1]).astype(jnp.bfloat16)
    up, down = powers_of(e_ref[...])
    for j in range(e_ref.shape[1]):
        cols = slice(j * BLK, (j + 1) * BLK)
        codes = w_ref[:, cols].astype(jnp.float32) * up[:, j : j + 1]
        levels = jnp.clip(jnp.floor(codes + 0.5), -8.0, 7.0)
        wq[:, cols] = (levels * down[:, j : j + 1]).astype(jnp.bfloat16)
    acc[...] += jnp.dot(sg[...], wq[...], preferred_element_type=jnp.float32)
    part_ref[...] = lax.dot_general(
        sg[...], x_ref[...], (((0,), (0,)), ((), ())), preferred_element_type=jnp.float32
    ).astype(jnp.bfloat16)

    @pl.when(step == pl.num_programs(0) - 1)
    def _():
        back_ref[...] = acc[...].astype(jnp.bfloat16)


def keep_kernel(at_ref, s_ref, w_ref, e_ref, o_ref):
    up, _ = powers_of(e_ref[...])
    for j in range(e_ref.shape[1]):
        cols = slice(j * BLK, (j + 1) * BLK)
        codes = w_ref[:, cols].astype(jnp.float32) * up[:, j : j + 1]
        inside = ((codes >= -8.5) & (codes <= 7.5)).astype(jnp.float32)
        o_ref[:, cols] = s_ref[:, cols].astype(jnp.float32) * inside


def pick_slots(sources, capp, top, me, m_ref, sel, prob):
    slots, tok = m_ref.shape[2], sel.shape[2]
    places = lax.broadcasted_iota(jnp.int32, (capp, slots), 0) + me * capp
    slot = lax.broadcasted_iota(jnp.int32, (slots, tok), 0)
    first = lax.broadcasted_iota(jnp.int32, (slots, tok), 1) * top
    owner = ((slot >= first) & (slot < first + top)).astype(jnp.float32).astype(jnp.bfloat16)

    @pl.loop(0, sources)
    def _(s):
        here = (places == m_ref[s, 0:1, :].astype(jnp.int32)).astype(jnp.float32)
        sel[s] = jnp.dot(
            here.astype(jnp.bfloat16), owner, preferred_element_type=jnp.float32
        ).astype(jnp.bfloat16)
        weight = jnp.sum(here * m_ref[s, 1:2, :], axis=1, keepdims=True)
        prob[s] = jnp.broadcast_to(weight, prob.shape[1:])


def share_kernel(sources, capp, top, at_ref, m_ref, g_ref, x_ref, w_ref, e_ref, back_ref, o_ref, sel, prob, sg, wq, acc):
    step = pl.program_id(0)
    tok = g_ref.shape[0] // sources

    @pl.when(step == 0)
    def _():
        acc[...] = jnp.zeros_like(acc)
        pick_slots(sources, capp, top, at_ref[1], m_ref, sel, prob)

    for s in range(sources):
        picked = jnp.dot(sel[s], g_ref[s * tok : (s + 1) * tok, :], preferred_element_type=jnp.float32)
        sg[s * capp : (s + 1) * capp, :] = (picked * prob[s][:, 0:1]).astype(jnp.bfloat16)
    grads = lax.dot_general(
        sg[...], x_ref[...], (((0,), (0,)), ((), ())), preferred_element_type=jnp.float32
    )
    up, down = powers_of(e_ref[...])
    for j in range(e_ref.shape[1]):
        cols = slice(j * BLK, (j + 1) * BLK)
        codes = w_ref[:, cols].astype(jnp.float32) * up[:, j : j + 1]
        levels = jnp.clip(jnp.floor(codes + 0.5), -8.0, 7.0)
        wq[:, cols] = (levels * down[:, j : j + 1]).astype(jnp.bfloat16)
        inside = ((codes >= -8.5) & (codes <= 7.5)).astype(jnp.float32)
        o_ref[:, cols] = grads[:, cols] * inside
    acc[...] += jnp.dot(sg[...], wq[...], preferred_element_type=jnp.float32)

    @pl.when(step == pl.num_programs(0) - 1)
    def _():
        back_ref[...] = acc[...].astype(jnp.bfloat16)


def pack(n, capp, route_probs, expert_ids, saved_inputs):
    tok, top = expert_ids.shape
    slots, hidden = tok * top, saved_inputs.shape[2]
    vmem = pl.BlockSpec(memory_space=pltpu.VMEM)
    return pl.pallas_call(
        functools.partial(pack_kernel, n, capp),
        out_shape=(
            jax.ShapeDtypeStruct((n, capp, hidden), jnp.bfloat16),
            jax.ShapeDtypeStruct((8, slots), jnp.float32),
        ),
        in_specs=[vmem] * 3,
        out_specs=(vmem, vmem),
        compiler_params=pltpu.CompilerParams(vmem_limit_bytes=VMEM_LIMIT),
        name="pack_slots",
    )(expert_ids.reshape(1, slots), route_probs.reshape(1, slots), saved_inputs.reshape(slots, hidden))


def local_shares(out_grads, route_probs, expert_ids, saved_inputs, w_latent, block_exponents):
    dp, n = lax.axis_size("dp"), lax.axis_size("expert")
    tok, top = expert_ids.shape
    width = out_grads.shape[1]
    hidden = saved_inputs.shape[2]
    slots = tok * top
    capp = -(-(tok * top * 3 // (2 * n)) // 16) * 16
    blocks = block_exponents.shape[2]
    bf16, f32 = jnp.bfloat16, jnp.float32
    share, depth, sources = width // dp, n // PLANE, dp * n
    vmem = pl.BlockSpec(memory_space=pltpu.VMEM)
    anyspace = pl.BlockSpec(memory_space=pl.ANY)
    dma = pltpu.SemaphoreType.DMA

    own = out_grads.reshape(tok, dp, share).transpose(1, 0, 2)
    sends, meta = pack(n, capp, route_probs, expert_ids, saved_inputs)
    g, x, m = pl.pallas_call(
        functools.partial(gather_kernel, dp, n),
        out_shape=(
            jax.ShapeDtypeStruct((dp, n, tok, share), bf16),
            jax.ShapeDtypeStruct((dp, n, capp, hidden), bf16),
            jax.ShapeDtypeStruct((dp, n, 8, slots), f32),
        ),
        in_specs=[anyspace] * 3,
        out_specs=(anyspace,) * 3,
        scratch_shapes=[
            dma((3,)),
            dma((dp,)),
            dma((depth, dp)),
            dma((depth, dp)),
            dma((depth, dp)),
            dma((2 * depth, dp)),
            dma((n,)),
            dma((dp, n)),
            dma((n,)),
            dma((dp, n)),
            dma((dp, n)),
            dma((dp, n)),
            dma((dp, n)),
        ],
        compiler_params=pltpu.CompilerParams(collective_id=0, has_side_effects=True),
        name="gather",
    )(own, sends, meta)

    tile = SHARE_TILE
    tiles = share // tile
    at = jnp.stack([lax.axis_index("dp") * tiles, lax.axis_index("expert")]).astype(jnp.int32)
    back, weight_grads = pl.pallas_call(
        functools.partial(share_kernel, sources, capp, top),
        grid_spec=pltpu.PrefetchScalarGridSpec(
            num_scalar_prefetch=1,
            grid=(tiles,),
            in_specs=[
                pl.BlockSpec((sources, 8, slots), lambda i, at: (0, 0, 0)),
                pl.BlockSpec((sources * tok, tile), lambda i, at: (0, i)),
                pl.BlockSpec((sources * capp, hidden), lambda i, at: (0, 0)),
                pl.BlockSpec((tile, hidden), lambda i, at: (at[0] + i, 0)),
                pl.BlockSpec((tile, blocks), lambda i, at: (at[0] + i, 0)),
            ],
            out_specs=(
                pl.BlockSpec((sources * capp, hidden), lambda i, at: (0, 0)),
                pl.BlockSpec((tile, hidden), lambda i, at: (i, 0)),
            ),
            scratch_shapes=[
                pltpu.VMEM((sources, capp, tok), bf16),
                pltpu.VMEM((sources, capp, 128), f32),
                pltpu.VMEM((sources * capp, tile), bf16),
                pltpu.VMEM((tile, hidden), bf16),
                pltpu.VMEM((sources * capp, hidden), f32),
            ],
        ),
        out_shape=(
            jax.ShapeDtypeStruct((sources * capp, hidden), bf16),
            jax.ShapeDtypeStruct((share, hidden), f32),
        ),
        compiler_params=pltpu.CompilerParams(vmem_limit_bytes=VMEM_LIMIT),
        name="share",
    )(at, m.reshape(sources, 8, slots), g.reshape(sources * tok, share), x.reshape(sources * capp, hidden),
      w_latent[0], block_exponents[0])

    returned = pl.pallas_call(
        functools.partial(return_kernel, dp, n),
        out_shape=jax.ShapeDtypeStruct((n, capp, hidden), bf16),
        in_specs=[vmem],
        out_specs=anyspace,
        scratch_shapes=[
            pltpu.VMEM((dp - 1, n, capp, hidden), bf16),
            pltpu.VMEM((n, capp, hidden), bf16),
            dma((dp - 1, depth)),
            dma((dp - 1, depth)),
            dma((1,)),
            dma((n,)),
            dma((n,)),
        ],
        compiler_params=pltpu.CompilerParams(
            collective_id=1, has_side_effects=True, vmem_limit_bytes=VMEM_LIMIT
        ),
        name="give_back",
    )(back.reshape(dp, n, capp, hidden))
    target = meta[0].astype(jnp.int32)
    input_grads = returned.reshape(n * capp, hidden)[target].reshape(tok, top, hidden)
    return (input_grads, weight_grads[None])


def tile_of(size, most):
    return max(t for t in range(16, most + 1, 16) if size % t == 0)


def local(out_grads, route_probs, expert_ids, saved_inputs, w_latent, block_exponents):
    n = lax.axis_size("expert")
    tok, top = expert_ids.shape
    width = out_grads.shape[1]
    hidden = saved_inputs.shape[2]
    slots = tok * top
    capacity = tok * top * 3 // (2 * n)
    capp = -(-capacity // 16) * 16
    blocks = block_exponents.shape[2]
    bf16, f32 = jnp.bfloat16, jnp.float32
    vmem = pl.BlockSpec(memory_space=pltpu.VMEM)
    anyspace = pl.BlockSpec(memory_space=pl.ANY)
    params = functools.partial(pltpu.CompilerParams, vmem_limit_bytes=VMEM_LIMIT)

    sends, meta = pl.pallas_call(
        functools.partial(pack_kernel, n, capp),
        out_shape=(
            jax.ShapeDtypeStruct((n, capp, hidden), bf16),
            jax.ShapeDtypeStruct((8, slots), f32),
        ),
        in_specs=[vmem] * 3,
        out_specs=(vmem, vmem),
        compiler_params=params(),
        name="pack_slots",
    )(expert_ids.reshape(1, slots), route_probs.reshape(1, slots), saved_inputs.reshape(slots, hidden))

    depth = n // PLANE
    dma = pltpu.SemaphoreType.DMA
    g, x, m = pl.pallas_call(
        functools.partial(exchange_kernel, n),
        out_shape=(
            jax.ShapeDtypeStruct((n, tok, width), bf16),
            jax.ShapeDtypeStruct((n, capp, hidden), bf16),
            jax.ShapeDtypeStruct((n, 8, slots), f32),
        ),
        in_specs=[anyspace] * 3,
        out_specs=(anyspace,) * 3,
        scratch_shapes=[
            dma((3,)),
            dma((depth, PIECES)),
            dma((depth, PIECES)),
            dma((depth, PIECES)),
            dma((2 * depth, PIECES)),
            dma((n,)),
            dma((n,)),
            dma((n,)),
            dma((n,)),
            dma((n, PIECES)),
        ],
        compiler_params=pltpu.CompilerParams(collective_id=0, has_side_effects=True),
        name="exchange",
    )(out_grads, sends, meta)

    me = lax.axis_index("expert").astype(jnp.int32).reshape(1)
    chunk = 512
    back, partial = pl.pallas_call(
        functools.partial(expert_kernel, n, capp, top),
        grid=(width // chunk,),
        out_shape=(
            jax.ShapeDtypeStruct((n * capp, hidden), bf16),
            jax.ShapeDtypeStruct((width, hidden), bf16),
        ),
        in_specs=[
            pl.BlockSpec(memory_space=pltpu.SMEM),
            pl.BlockSpec((n, 8, slots), lambda i: (0, 0, 0)),
            pl.BlockSpec((n * tok, chunk), lambda i: (0, i)),
            pl.BlockSpec((n * capp, hidden), lambda i: (0, 0)),
            pl.BlockSpec((chunk, hidden), lambda i: (i, 0)),
            pl.BlockSpec((chunk, blocks), lambda i: (i, 0)),
        ],
        out_specs=(
            pl.BlockSpec((n * capp, hidden), lambda i: (0, 0)),
            pl.BlockSpec((chunk, hidden), lambda i: (i, 0)),
        ),
        scratch_shapes=[
            pltpu.VMEM((n, capp, tok), bf16),
            pltpu.VMEM((n, capp, 128), f32),
            pltpu.VMEM((n * capp, chunk), bf16),
            pltpu.VMEM((chunk, hidden), bf16),
            pltpu.VMEM((n * capp, hidden), f32),
        ],
        compiler_params=params(),
        name="expert",
    )(me, m, g.reshape(n * tok, width), x.reshape(n * capp, hidden), w_latent[0], block_exponents[0])

    returned = lax.all_to_all(
        back.reshape(n, capp, hidden), "expert", split_axis=0, concat_axis=0, tiled=True
    )
    target = meta[0].astype(jnp.int32)
    input_grads = returned.reshape(n * capp, hidden)[target].reshape(tok, top, hidden)

    summed = lax.psum_scatter(partial, "dp", scatter_dimension=0, tiled=True)
    share = summed.shape[0]
    tile = tile_of(share, 256)
    tiles = share // tile
    at = (lax.axis_index("dp") * tiles).astype(jnp.int32).reshape(1)
    weight_grads = pl.pallas_call(
        keep_kernel,
        grid_spec=pltpu.PrefetchScalarGridSpec(
            num_scalar_prefetch=1,
            grid=(tiles,),
            in_specs=[
                pl.BlockSpec((tile, hidden), lambda i, at: (i, 0)),
                pl.BlockSpec((tile, hidden), lambda i, at: (at[0] + i, 0)),
                pl.BlockSpec((tile, blocks), lambda i, at: (at[0] + i, 0)),
            ],
            out_specs=pl.BlockSpec((tile, hidden), lambda i, at: (i, 0)),
        ),
        out_shape=jax.ShapeDtypeStruct((share, hidden), f32),
        compiler_params=params(),
        name="keep",
    )(at, summed, w_latent[0], block_exponents[0])
    return (input_grads, weight_grads[None])


def solution(mesh):
    placed = (
        P(("dp", "expert"), None),
        P(("dp", "expert"), None),
        P(("dp", "expert"), None),
        P(("dp", "expert"), None, None),
        P("expert", None, None),
        P("expert", None, None),
    )
    dp = mesh.shape["dp"]

    def body(out_grads, *rest):
        share = out_grads.shape[1] // dp
        plan = local_shares if dp == 2 and share % SHARE_TILE == 0 else local
        return plan(out_grads, *rest)

    return jax.shard_map(
        body,
        mesh=mesh,
        in_specs=placed,
        out_specs=(P(("dp", "expert"), None, None), P("expert", "dp", None)),
        check_vma=False,
    )
```

```python
import functools

import jax
import jax.numpy as jnp
from jax import lax
from jax.experimental import pallas as pl
from jax.experimental.pallas import tpu as pltpu
from jax.sharding import PartitionSpec as P

BLK = 128
PLANE = 4
PIECES = 2
VMEM_LIMIT = 56 * 1024 * 1024
SHARE_TILE = 256


def pack_kernel(n, capp, ids_ref, probs_ref, saved_ref, send_ref, meta_ref):
    slots = ids_ref.shape[1]
    ids = ids_ref[...]
    expert_rows = lax.broadcasted_iota(jnp.int32, (n, slots), 0)
    onehot = (expert_rows == ids).astype(jnp.float32)
    earlier = lax.broadcasted_iota(jnp.int32, (slots, slots), 0)
    later = lax.broadcasted_iota(jnp.int32, (slots, slots), 1)
    before = jnp.dot(
        onehot.astype(jnp.bfloat16),
        (earlier < later).astype(jnp.float32).astype(jnp.bfloat16),
        preferred_element_type=jnp.float32,
    )
    position = jnp.sum(before * onehot, axis=0, keepdims=True)
    target = ids.astype(jnp.float32) * float(capp) + position
    meta_ref[...] = jnp.zeros_like(meta_ref)
    meta_ref[0:1, :] = target
    meta_ref[1:2, :] = probs_ref[...]
    target = target.astype(jnp.int32)
    places = lax.broadcasted_iota(jnp.int32, (capp, slots), 0)

    @pl.loop(0, n)
    def _(e):
        pick = (places + e * capp == target).astype(jnp.float32).astype(jnp.bfloat16)
        send_ref[e] = jnp.dot(pick, saved_ref[...], preferred_element_type=jnp.float32).astype(
            jnp.bfloat16
        )


def exchange_kernel(
    n, own, xs, meta, g, x, m, local_sem, up_sem, down_sem, y_sem, core_sem, x_send, x_recv, m_send, m_recv, g_recv
):
    me = lax.axis_index("expert")
    depth = n // PLANE
    z = me // PLANE
    lane = lax.rem(me, PLANE)
    core_lane = lane + 1 - 2 * lax.rem(lane, 2)
    y_lane = lax.rem(lane + 2, PLANE)
    core_mate = z * PLANE + core_lane
    y_mate = z * PLANE + y_lane
    rows = own.shape[0] // PIECES

    barrier = pltpu.get_barrier_semaphore()
    for d in range(1, n):
        pl.semaphore_signal(barrier, inc=1, device_id={"expert": lax.rem(me + d, n)})
    pl.semaphore_wait(barrier, n - 1)

    def cp(block, k, dest, send, from_own=False):
        part = pl.ds(k * rows, rows)
        return pltpu.make_async_remote_copy(
            src_ref=own.at[part] if from_own else g.at[block, part],
            dst_ref=g.at[block, part],
            send_sem=send,
            recv_sem=g_recv.at[block, k],
            device_id={"expert": dest},
        )

    def got(block, k):
        cp(block, k, me, up_sem.at[0, k]).wait_recv()

    def hand_on(bz, k, up, down, from_own=False):
        block = bz * PLANE + lane
        if up:
            @pl.when(z + 1 < depth)
            def _():
                cp(block, k, me + PLANE, up_sem.at[bz, k], from_own).start()
        if down:
            @pl.when(z >= 1)
            def _():
                cp(block, k, me - PLANE, down_sem.at[bz, k], from_own).start()
        cp(block, k, y_mate, y_sem.at[bz, k], from_own).start()
        cp(block, k, core_mate, core_sem.at[bz, k], from_own).start()

    for k in range(PIECES):
        hand_on(z, k, True, True, from_own=True)

    locals_ = [
        pltpu.make_async_copy(own, g.at[me], local_sem.at[0]),
        pltpu.make_async_copy(xs.at[me], x.at[me], local_sem.at[1]),
        pltpu.make_async_copy(meta, m.at[me], local_sem.at[2]),
    ]
    for c in locals_:
        c.start()

    def xcp(d):
        dest = lax.rem(me + d, n)
        return pltpu.make_async_remote_copy(
            src_ref=xs.at[dest], dst_ref=x.at[me], send_sem=x_send.at[d], recv_sem=x_recv.at[me],
            device_id={"expert": dest},
        )

    def mcp(d):
        return pltpu.make_async_remote_copy(
            src_ref=meta, dst_ref=m.at[me], send_sem=m_send.at[d], recv_sem=m_recv.at[me],
            device_id={"expert": lax.rem(me + d, n)},
        )

    for d in range(1, n):
        mcp(d).start()
        xcp(d).start()

    def relay(bz, k):
        block = bz * PLANE + y_lane
        got(block, k)
        cp(block, k, core_mate, core_sem.at[depth + bz, k]).start()

    for step in range(1, depth + 1):
        for k in range(PIECES):
            if step < depth:
                @pl.when(z - step >= 0)
                def _():
                    got((z - step) * PLANE + lane, k)
                    hand_on(z - step, k, True, False)

                @pl.when(z + step < depth)
                def _():
                    got((z + step) * PLANE + lane, k)
                    hand_on(z + step, k, False, True)
            last = step - 1
            @pl.when(z - last >= 0)
            def _():
                relay(z - last, k)

            if last:
                @pl.when(z + last < depth)
                def _():
                    relay(z + last, k)

    for bz in range(depth):
        for k in range(PIECES):
            got(bz * PLANE + core_lane, k)
            got(bz * PLANE + lax.rem(core_lane + 2, PLANE), k)
    for d in range(1, n):
        peer = lax.rem(me + d, n)
        pltpu.make_async_remote_copy(
            src_ref=xs.at[peer], dst_ref=x.at[peer], send_sem=x_send.at[d], recv_sem=x_recv.at[peer],
            device_id={"expert": peer},
        ).wait_recv()
        pltpu.make_async_remote_copy(
            src_ref=meta, dst_ref=m.at[peer], send_sem=m_send.at[d], recv_sem=m_recv.at[peer],
            device_id={"expert": peer},
        ).wait_recv()
    for d in range(1, n):
        xcp(d).wait_send()
        mcp(d).wait_send()
    for bz in range(depth):
        for k in range(PIECES):
            block = bz * PLANE + lane

            @pl.when((z + 1 < depth) & (bz <= z))
            def _():
                cp(block, k, me, up_sem.at[bz, k]).wait_send()

            @pl.when((z >= 1) & (bz >= z))
            def _():
                cp(block, k, me, down_sem.at[bz, k]).wait_send()

            cp(block, k, y_mate, y_sem.at[bz, k]).wait_send()
            cp(block, k, core_mate, core_sem.at[bz, k]).wait_send()
            cp(block, k, core_mate, core_sem.at[depth + bz, k]).wait_send()
    for c in locals_:
        c.wait()


def gather_kernel(
    dp, n, own, ids, probs, saved, g, x, m, meta, xs, local_sem, a_send, up_sem, down_sem, y_sem, core_sem,
    x_send, x_recv, m_send, m_recv, g_recv, fx_send, fm_send
):
    me = lax.axis_index("expert")
    r = lax.axis_index("dp")
    depth = n // PLANE
    z = me // PLANE
    lane = lax.rem(me, PLANE)
    core_lane = lane + 1 - 2 * lax.rem(lane, 2)
    y_lane = lax.rem(lane + 2, PLANE)
    core_mate = z * PLANE + core_lane
    y_mate = z * PLANE + y_lane
    reps = [lax.rem(r + k, dp) for k in range(dp)]
    rows, share = own.shape[0] // PIECES, own.shape[1] // dp

    def own_part(rep, p):
        return own.at[pl.ds(p * rows, rows), pl.ds(pl.multiple_of(rep * share, BLK), share)]

    def g_part(rep, block, p):
        return g.at[rep, block, pl.ds(p * rows, rows)]

    barrier = pltpu.get_barrier_semaphore()
    for d in range(1, n):
        pl.semaphore_signal(barrier, inc=1, device_id={"expert": lax.rem(me + d, n)})
    for k in range(1, dp):
        pl.semaphore_signal(barrier, inc=1, device_id={"dp": reps[k]})
    pl.semaphore_wait(barrier, n - 1 + dp - 1)

    def across(k, p):
        return pltpu.make_async_remote_copy(
            src_ref=own_part(reps[k], p), dst_ref=g_part(r, me, p), send_sem=a_send.at[k, p],
            recv_sem=g_recv.at[r, me, p], device_id={"dp": reps[k]},
        )

    def cp(block, k, p, dest, send, from_own=False):
        return pltpu.make_async_remote_copy(
            src_ref=own_part(r, p) if from_own else g_part(reps[k], block, p),
            dst_ref=g_part(reps[k], block, p),
            send_sem=send,
            recv_sem=g_recv.at[reps[k], block, p],
            device_id={"expert": dest},
        )

    def got(block, k, p):
        cp(block, k, p, me, up_sem.at[0, k, p]).wait_recv()

    def hand_on(bz, k, p, up, down, from_own=False):
        block = bz * PLANE + lane
        if up:
            @pl.when(z + 1 < depth)
            def _():
                cp(block, k, p, me + PLANE, up_sem.at[bz, k, p], from_own).start()
        if down:
            @pl.when(z >= 1)
            def _():
                cp(block, k, p, me - PLANE, down_sem.at[bz, k, p], from_own).start()
        cp(block, k, p, y_mate, y_sem.at[bz, k, p], from_own).start()
        cp(block, k, p, core_mate, core_sem.at[bz, k, p], from_own).start()

    for p in range(PIECES):
        for k in range(1, dp):
            across(k, p).start()
        hand_on(z, 0, p, True, True, from_own=True)
    pack_kernel(n, xs.shape[1], ids, probs, saved, xs, meta)

    locals_ = [
        pltpu.make_async_copy(
            own.at[:, pl.ds(pl.multiple_of(r * share, BLK), share)], g.at[r, me], local_sem.at[0]
        ),
        pltpu.make_async_copy(xs.at[me], x.at[r, me], local_sem.at[1]),
        pltpu.make_async_copy(meta, m.at[r, me], local_sem.at[2]),
    ]
    for c in locals_:
        c.start()

    def xcp(d):
        dest = lax.rem(me + d, n)
        return pltpu.make_async_remote_copy(
            src_ref=xs.at[dest], dst_ref=x.at[r, me], send_sem=x_send.at[d], recv_sem=x_recv.at[r, me],
            device_id={"expert": dest},
        )

    def mcp(d):
        return pltpu.make_async_remote_copy(
            src_ref=meta, dst_ref=m.at[r, me], send_sem=m_send.at[d], recv_sem=m_recv.at[r, me],
            device_id={"expert": lax.rem(me + d, n)},
        )

    for d in range(1, n):
        mcp(d).start()
        xcp(d).start()

    def forward(s, k, own_block=False):
        return (
            pltpu.make_async_remote_copy(
                src_ref=xs.at[s] if own_block else x.at[r, s], dst_ref=x.at[r, s],
                send_sem=fx_send.at[k, s], recv_sem=x_recv.at[r, s], device_id={"dp": reps[k]},
            ),
            pltpu.make_async_remote_copy(
                src_ref=meta if own_block else m.at[r, s], dst_ref=m.at[r, s],
                send_sem=fm_send.at[k, s], recv_sem=m_recv.at[r, s], device_id={"dp": reps[k]},
            ),
        )

    def arrived(rep, s):
        pltpu.make_async_remote_copy(
            src_ref=x.at[rep, s], dst_ref=x.at[rep, s], send_sem=x_send.at[0], recv_sem=x_recv.at[rep, s],
            device_id={"dp": r},
        ).wait_recv()
        pltpu.make_async_remote_copy(
            src_ref=m.at[rep, s], dst_ref=m.at[rep, s], send_sem=m_send.at[0], recv_sem=m_recv.at[rep, s],
            device_id={"dp": r},
        ).wait_recv()

    def slots_of_plane(pz):
        for i in range(PLANE):
            arrived(r, pz * PLANE + i)
            for k in range(1, dp):
                for c in forward(pz * PLANE + i, k):
                    c.start()

    for k in range(1, dp):
        for c in forward(me, k, True):
            c.start()
        for p in range(PIECES):
            got(me, k, p)
            hand_on(z, k, p, True, True)

    def relay(bz, k, p):
        block = bz * PLANE + y_lane
        got(block, k, p)
        cp(block, k, p, core_mate, core_sem.at[depth + bz, k, p]).start()

    both = [(k, p) for k in range(dp) for p in range(PIECES)]
    for step in range(1, depth + 1):
        last = step - 1
        for k, p in both:
            if step < depth:
                @pl.when(z - step >= 0)
                def _():
                    got((z - step) * PLANE + lane, k, p)
                    hand_on(z - step, k, p, True, False)

                @pl.when(z + step < depth)
                def _():
                    got((z + step) * PLANE + lane, k, p)
                    hand_on(z + step, k, p, False, True)
            @pl.when(z - last >= 0)
            def _():
                relay(z - last, k, p)

            if last:
                @pl.when(z + last < depth)
                def _():
                    relay(z + last, k, p)
        if last == 0:
            for i in range(1, PLANE):
                s = z * PLANE + lax.rem(lane + i, PLANE)
                arrived(r, s)
                for k in range(1, dp):
                    for c in forward(s, k):
                        c.start()
        else:
            @pl.when(z - last >= 0)
            def _():
                slots_of_plane(z - last)

            @pl.when(z + last < depth)
            def _():
                slots_of_plane(z + last)

    for bz in range(depth):
        for k, p in both:
            got(bz * PLANE + core_lane, k, p)
            got(bz * PLANE + lax.rem(core_lane + 2, PLANE), k, p)
    for k in range(1, dp):
        for s in range(n):
            arrived(reps[k], s)
    for d in range(1, n):
        xcp(d).wait_send()
        mcp(d).wait_send()
    for k in range(1, dp):
        for p in range(PIECES):
            across(k, p).wait_send()
        for s in range(n):
            for c in forward(s, k):
                c.wait_send()
    for bz in range(depth):
        for k, p in both:
            block = bz * PLANE + lane

            @pl.when((z + 1 < depth) & (bz <= z))
            def _():
                cp(block, k, p, me, up_sem.at[bz, k, p]).wait_send()

            @pl.when((z >= 1) & (bz >= z))
            def _():
                cp(block, k, p, me, down_sem.at[bz, k, p]).wait_send()

            cp(block, k, p, y_mate, y_sem.at[bz, k, p]).wait_send()
            cp(block, k, p, core_mate, core_sem.at[bz, k, p]).wait_send()
            cp(block, k, p, core_mate, core_sem.at[depth + bz, k, p]).wait_send()
    for c in locals_:
        c.wait()


def return_kernel(dp, n, part, ret, inbox, total, a_send, a_recv, local_sem, send, recv):
    me = lax.axis_index("expert")
    r = lax.axis_index("dp")
    depth = n // PLANE
    z = me // PLANE
    lane = lax.rem(me, PLANE)
    reps = [lax.rem(r + k, dp) for k in range(dp)]
    order = sorted(range(1, depth), key=lambda o: abs(2 * o - depth)) + [0]
    half = PLANE // 2
    groups = [lax.rem(z + o, depth) * PLANE + h for o in order for h in (0, half)]
    count = len(groups)

    barrier = pltpu.get_barrier_semaphore()
    for d in range(1, n):
        pl.semaphore_signal(barrier, inc=1, device_id={"expert": lax.rem(me + d, n)})
    for k in range(1, dp):
        pl.semaphore_signal(barrier, inc=1, device_id={"dp": reps[k]})
    pl.semaphore_wait(barrier, n - 1 + dp - 1)

    def across(i, k):
        return pltpu.make_async_remote_copy(
            src_ref=part.at[reps[k], pl.ds(groups[i], half)],
            dst_ref=inbox.at[dp - k - 1, pl.ds(groups[i], half)],
            send_sem=a_send.at[k - 1, i],
            recv_sem=a_recv.at[dp - k - 1, i],
            device_id={"dp": reps[k]},
        )

    def back(dest):
        return pltpu.make_async_remote_copy(
            src_ref=total.at[dest], dst_ref=ret.at[me], send_sem=send.at[dest], recv_sem=recv.at[me],
            device_id={"expert": dest},
        )

    for i in range(count):
        for k in range(1, dp):
            across(i, k).start()
    for i in range(count):
        for k in range(1, dp):
            across(i, k).wait_recv()
        for j in range(half):
            row = groups[i] + j
            value = part[r, row].astype(jnp.float32)
            for k in range(1, dp):
                value = value + inbox[k - 1, row].astype(jnp.float32)
            total[row] = value.astype(jnp.bfloat16)
        if i < count - 2:
            for j in range(half):
                back(groups[i] + j).start()
    for j in range(1, PLANE):
        back(z * PLANE + lax.rem(lane + j, PLANE)).start()
    mine = pltpu.make_async_copy(total.at[me], ret.at[me], local_sem.at[0])
    mine.start()
    for d in range(1, n):
        peer = lax.rem(me + d, n)
        pltpu.make_async_remote_copy(
            src_ref=total.at[peer], dst_ref=ret.at[peer], send_sem=send.at[peer], recv_sem=recv.at[peer],
            device_id={"expert": peer},
        ).wait_recv()
    for d in range(1, n):
        back(lax.rem(me + d, n)).wait_send()
    for i in range(count):
        for k in range(1, dp):
            across(i, k).wait_send()
    mine.wait()


def powers_of(exponents):
    one = jnp.ones_like(exponents)
    up = jnp.left_shift(one, -exponents).astype(jnp.float32)
    down = jnp.left_shift(one, exponents + 16).astype(jnp.float32) * (2.0**-16)
    return up, down


def expert_kernel(n, capp, top, me_ref, m_ref, g_ref, x_ref, w_ref, e_ref, back_ref, part_ref, sel, prob, sg, wq, acc):
    step = pl.program_id(0)
    tok = g_ref.shape[0] // n
    slots = m_ref.shape[2]

    @pl.when(step == 0)
    def _():
        acc[...] = jnp.zeros_like(acc)
        places = lax.broadcasted_iota(jnp.int32, (capp, slots), 0) + me_ref[0] * capp
        token_of = lax.broadcasted_iota(jnp.int32, (slots, tok), 0)
        first = lax.broadcasted_iota(jnp.int32, (slots, tok), 1) * top
        owner = ((token_of >= first) & (token_of < first + top)).astype(jnp.float32).astype(jnp.bfloat16)

        @pl.loop(0, n)
        def _(s):
            here = (places == m_ref[s, 0:1, :].astype(jnp.int32)).astype(jnp.float32)
            sel[s] = jnp.dot(
                here.astype(jnp.bfloat16), owner, preferred_element_type=jnp.float32
            ).astype(jnp.bfloat16)
            weight = jnp.sum(here * m_ref[s, 1:2, :], axis=1, keepdims=True)
            prob[s] = jnp.broadcast_to(weight, prob.shape[1:])

    for s in range(n):
        picked = jnp.dot(sel[s], g_ref[s * tok : (s + 1) * tok, :], preferred_element_type=jnp.float32)
        sg[s * capp : (s + 1) * capp, :] = (picked * prob[s][:, 0:1]).astype(jnp.bfloat16)
    up, down = powers_of(e_ref[...])
    for j in range(e_ref.shape[1]):
        cols = slice(j * BLK, (j + 1) * BLK)
        codes = w_ref[:, cols].astype(jnp.float32) * up[:, j : j + 1]
        levels = jnp.clip(jnp.floor(codes + 0.5), -8.0, 7.0)
        wq[:, cols] = (levels * down[:, j : j + 1]).astype(jnp.bfloat16)
    acc[...] += jnp.dot(sg[...], wq[...], preferred_element_type=jnp.float32)
    part_ref[...] = lax.dot_general(
        sg[...], x_ref[...], (((0,), (0,)), ((), ())), preferred_element_type=jnp.float32
    ).astype(jnp.bfloat16)

    @pl.when(step == pl.num_programs(0) - 1)
    def _():
        back_ref[...] = acc[...].astype(jnp.bfloat16)


def keep_kernel(at_ref, s_ref, w_ref, e_ref, o_ref):
    up, _ = powers_of(e_ref[...])
    for j in range(e_ref.shape[1]):
        cols = slice(j * BLK, (j + 1) * BLK)
        codes = w_ref[:, cols].astype(jnp.float32) * up[:, j : j + 1]
        inside = ((codes >= -8.5) & (codes <= 7.5)).astype(jnp.float32)
        o_ref[:, cols] = s_ref[:, cols].astype(jnp.float32) * inside


def pick_slots(sources, capp, tok, top, me, m_ref, sel, prob):
    slots = m_ref.shape[2]
    places = lax.broadcasted_iota(jnp.int32, (capp, slots), 0) + me * capp
    slot = lax.broadcasted_iota(jnp.int32, (slots, tok), 0)
    first = lax.broadcasted_iota(jnp.int32, (slots, tok), 1) * top
    owner = ((slot >= first) & (slot < first + top)).astype(jnp.float32).astype(jnp.bfloat16)

    @pl.loop(0, sources // 2)
    def _(pair):
        sel[pair] = jnp.zeros(sel.shape[1:], sel.dtype)
        for h in range(2):
            at = slice(h * capp, (h + 1) * capp)
            here = (places == m_ref[2 * pair + h, 0:1, :].astype(jnp.int32)).astype(jnp.float32)
            sel[pair, at, h * tok : (h + 1) * tok] = jnp.dot(
                here.astype(jnp.bfloat16), owner, preferred_element_type=jnp.float32
            ).astype(jnp.bfloat16)
            weight = jnp.sum(here * m_ref[2 * pair + h, 1:2, :], axis=1, keepdims=True)
            prob[pair, at, :] = jnp.broadcast_to(weight, (capp, prob.shape[2]))


def share_kernel(sources, capp, top, at_ref, m_ref, g_ref, x_ref, w_ref, e_ref, back_ref, o_ref, sel, prob, sg, wq, acc):
    step = pl.program_id(0)
    tok = g_ref.shape[0] // sources

    @pl.when(step == 0)
    def _():
        acc[...] = jnp.zeros_like(acc)
        pick_slots(sources, capp, tok, top, at_ref[1], m_ref, sel, prob)

    for s in range(sources // 2):
        pair = slice(2 * s * tok, 2 * (s + 1) * tok)
        picked = jnp.dot(sel[s], g_ref[pair, :], preferred_element_type=jnp.float32)
        weight = jnp.concatenate([prob[s]] * (picked.shape[1] // prob.shape[2]), axis=1)
        sg[2 * s * capp : 2 * (s + 1) * capp, :] = (picked * weight).astype(jnp.bfloat16)
    grads = lax.dot_general(
        sg[...], x_ref[...], (((0,), (0,)), ((), ())), preferred_element_type=jnp.float32
    )
    up, down = powers_of(e_ref[...])
    for j in range(e_ref.shape[1]):
        cols = slice(j * BLK, (j + 1) * BLK)
        codes = w_ref[:, cols].astype(jnp.float32) * up[:, j : j + 1]
        levels = jnp.clip(jnp.floor(codes + 0.5), -8.0, 7.0)
        wq[:, cols] = (levels * down[:, j : j + 1]).astype(jnp.bfloat16)
        inside = ((codes >= -8.5) & (codes <= 7.5)).astype(jnp.float32)
        o_ref[:, cols] = grads[:, cols] * inside
    acc[...] += jnp.dot(sg[...], wq[...], preferred_element_type=jnp.float32)

    @pl.when(step == pl.num_programs(0) - 1)
    def _():
        back_ref[...] = acc[...].astype(jnp.bfloat16)


def pack(n, capp, route_probs, expert_ids, saved_inputs):
    tok, top = expert_ids.shape
    slots, hidden = tok * top, saved_inputs.shape[2]
    vmem = pl.BlockSpec(memory_space=pltpu.VMEM)
    return pl.pallas_call(
        functools.partial(pack_kernel, n, capp),
        out_shape=(
            jax.ShapeDtypeStruct((n, capp, hidden), jnp.bfloat16),
            jax.ShapeDtypeStruct((8, slots), jnp.float32),
        ),
        in_specs=[vmem] * 3,
        out_specs=(vmem, vmem),
        compiler_params=pltpu.CompilerParams(vmem_limit_bytes=VMEM_LIMIT),
        name="pack_slots",
    )(expert_ids.reshape(1, slots), route_probs.reshape(1, slots), saved_inputs.reshape(slots, hidden))


def local_shares(out_grads, route_probs, expert_ids, saved_inputs, w_latent, block_exponents):
    dp, n = lax.axis_size("dp"), lax.axis_size("expert")
    tok, top = expert_ids.shape
    width = out_grads.shape[1]
    hidden = saved_inputs.shape[2]
    slots = tok * top
    capp = -(-(tok * top * 3 // (2 * n)) // 16) * 16
    blocks = block_exponents.shape[2]
    bf16, f32 = jnp.bfloat16, jnp.float32
    share, depth, sources = width // dp, n // PLANE, dp * n
    vmem = pl.BlockSpec(memory_space=pltpu.VMEM)
    anyspace = pl.BlockSpec(memory_space=pl.ANY)
    dma = pltpu.SemaphoreType.DMA

    g, x, m, meta = pl.pallas_call(
        functools.partial(gather_kernel, dp, n),
        out_shape=(
            jax.ShapeDtypeStruct((dp, n, tok, share), bf16),
            jax.ShapeDtypeStruct((dp, n, capp, hidden), bf16),
            jax.ShapeDtypeStruct((dp, n, 8, slots), f32),
            jax.ShapeDtypeStruct((8, slots), f32),
        ),
        in_specs=[anyspace] + [vmem] * 3,
        out_specs=(anyspace,) * 3 + (vmem,),
        scratch_shapes=[
            pltpu.VMEM((n, capp, hidden), bf16),
            dma((3,)),
            dma((dp, PIECES)),
            dma((depth, dp, PIECES)),
            dma((depth, dp, PIECES)),
            dma((depth, dp, PIECES)),
            dma((2 * depth, dp, PIECES)),
            dma((n,)),
            dma((dp, n)),
            dma((n,)),
            dma((dp, n)),
            dma((dp, n, PIECES)),
            dma((dp, n)),
            dma((dp, n)),
        ],
        compiler_params=pltpu.CompilerParams(
            collective_id=0, has_side_effects=True, vmem_limit_bytes=VMEM_LIMIT
        ),
        name="gather",
    )(out_grads, expert_ids.reshape(1, slots), route_probs.reshape(1, slots), saved_inputs.reshape(slots, hidden))

    tile = SHARE_TILE
    tiles = share // tile
    at = jnp.stack([lax.axis_index("dp") * tiles, lax.axis_index("expert")]).astype(jnp.int32)
    back, weight_grads = pl.pallas_call(
        functools.partial(share_kernel, sources, capp, top),
        grid_spec=pltpu.PrefetchScalarGridSpec(
            num_scalar_prefetch=1,
            grid=(tiles,),
            in_specs=[
                pl.BlockSpec((sources, 8, slots), lambda i, at: (0, 0, 0)),
                pl.BlockSpec((sources * tok, tile), lambda i, at: (0, i)),
                pl.BlockSpec((sources * capp, hidden), lambda i, at: (0, 0)),
                pl.BlockSpec((tile, hidden), lambda i, at: (at[0] + i, 0)),
                pl.BlockSpec((tile, blocks), lambda i, at: (at[0] + i, 0)),
            ],
            out_specs=(
                pl.BlockSpec((sources * capp, hidden), lambda i, at: (0, 0)),
                pl.BlockSpec((tile, hidden), lambda i, at: (i, 0)),
            ),
            scratch_shapes=[
                pltpu.VMEM((sources // 2, 2 * capp, 2 * tok), bf16),
                pltpu.VMEM((sources // 2, 2 * capp, 128), f32),
                pltpu.VMEM((sources * capp, tile), bf16),
                pltpu.VMEM((tile, hidden), bf16),
                pltpu.VMEM((sources * capp, hidden), f32),
            ],
        ),
        out_shape=(
            jax.ShapeDtypeStruct((sources * capp, hidden), bf16),
            jax.ShapeDtypeStruct((share, hidden), f32),
        ),
        compiler_params=pltpu.CompilerParams(vmem_limit_bytes=VMEM_LIMIT),
        name="share",
    )(at, m.reshape(sources, 8, slots), g.reshape(sources * tok, share), x.reshape(sources * capp, hidden),
      w_latent[0], block_exponents[0])

    returned = pl.pallas_call(
        functools.partial(return_kernel, dp, n),
        out_shape=jax.ShapeDtypeStruct((n, capp, hidden), bf16),
        in_specs=[vmem],
        out_specs=anyspace,
        scratch_shapes=[
            pltpu.VMEM((dp - 1, n, capp, hidden), bf16),
            pltpu.VMEM((n, capp, hidden), bf16),
            dma((dp - 1, 2 * depth)),
            dma((dp - 1, 2 * depth)),
            dma((1,)),
            dma((n,)),
            dma((n,)),
        ],
        compiler_params=pltpu.CompilerParams(
            collective_id=1, has_side_effects=True, vmem_limit_bytes=VMEM_LIMIT
        ),
        name="give_back",
    )(back.reshape(dp, n, capp, hidden))
    target = meta[0].astype(jnp.int32)
    input_grads = returned.reshape(n * capp, hidden)[target].reshape(tok, top, hidden)
    return (input_grads, weight_grads[None])


def tile_of(size, most):
    return max(t for t in range(16, most + 1, 16) if size % t == 0)


def local(out_grads, route_probs, expert_ids, saved_inputs, w_latent, block_exponents):
    n = lax.axis_size("expert")
    tok, top = expert_ids.shape
    width = out_grads.shape[1]
    hidden = saved_inputs.shape[2]
    slots = tok * top
    capacity = tok * top * 3 // (2 * n)
    capp = -(-capacity // 16) * 16
    blocks = block_exponents.shape[2]
    bf16, f32 = jnp.bfloat16, jnp.float32
    vmem = pl.BlockSpec(memory_space=pltpu.VMEM)
    anyspace = pl.BlockSpec(memory_space=pl.ANY)
    params = functools.partial(pltpu.CompilerParams, vmem_limit_bytes=VMEM_LIMIT)

    sends, meta = pl.pallas_call(
        functools.partial(pack_kernel, n, capp),
        out_shape=(
            jax.ShapeDtypeStruct((n, capp, hidden), bf16),
            jax.ShapeDtypeStruct((8, slots), f32),
        ),
        in_specs=[vmem] * 3,
        out_specs=(vmem, vmem),
        compiler_params=params(),
        name="pack_slots",
    )(expert_ids.reshape(1, slots), route_probs.reshape(1, slots), saved_inputs.reshape(slots, hidden))

    depth = n // PLANE
    dma = pltpu.SemaphoreType.DMA
    g, x, m = pl.pallas_call(
        functools.partial(exchange_kernel, n),
        out_shape=(
            jax.ShapeDtypeStruct((n, tok, width), bf16),
            jax.ShapeDtypeStruct((n, capp, hidden), bf16),
            jax.ShapeDtypeStruct((n, 8, slots), f32),
        ),
        in_specs=[anyspace] * 3,
        out_specs=(anyspace,) * 3,
        scratch_shapes=[
            dma((3,)),
            dma((depth, PIECES)),
            dma((depth, PIECES)),
            dma((depth, PIECES)),
            dma((2 * depth, PIECES)),
            dma((n,)),
            dma((n,)),
            dma((n,)),
            dma((n,)),
            dma((n, PIECES)),
        ],
        compiler_params=pltpu.CompilerParams(collective_id=0, has_side_effects=True),
        name="exchange",
    )(out_grads, sends, meta)

    me = lax.axis_index("expert").astype(jnp.int32).reshape(1)
    chunk = 512
    back, partial = pl.pallas_call(
        functools.partial(expert_kernel, n, capp, top),
        grid=(width // chunk,),
        out_shape=(
            jax.ShapeDtypeStruct((n * capp, hidden), bf16),
            jax.ShapeDtypeStruct((width, hidden), bf16),
        ),
        in_specs=[
            pl.BlockSpec(memory_space=pltpu.SMEM),
            pl.BlockSpec((n, 8, slots), lambda i: (0, 0, 0)),
            pl.BlockSpec((n * tok, chunk), lambda i: (0, i)),
            pl.BlockSpec((n * capp, hidden), lambda i: (0, 0)),
            pl.BlockSpec((chunk, hidden), lambda i: (i, 0)),
            pl.BlockSpec((chunk, blocks), lambda i: (i, 0)),
        ],
        out_specs=(
            pl.BlockSpec((n * capp, hidden), lambda i: (0, 0)),
            pl.BlockSpec((chunk, hidden), lambda i: (i, 0)),
        ),
        scratch_shapes=[
            pltpu.VMEM((n, capp, tok), bf16),
            pltpu.VMEM((n, capp, 128), f32),
            pltpu.VMEM((n * capp, chunk), bf16),
            pltpu.VMEM((chunk, hidden), bf16),
            pltpu.VMEM((n * capp, hidden), f32),
        ],
        compiler_params=params(),
        name="expert",
    )(me, m, g.reshape(n * tok, width), x.reshape(n * capp, hidden), w_latent[0], block_exponents[0])

    returned = lax.all_to_all(
        back.reshape(n, capp, hidden), "expert", split_axis=0, concat_axis=0, tiled=True
    )
    target = meta[0].astype(jnp.int32)
    input_grads = returned.reshape(n * capp, hidden)[target].reshape(tok, top, hidden)

    summed = lax.psum_scatter(partial, "dp", scatter_dimension=0, tiled=True)
    share = summed.shape[0]
    tile = tile_of(share, 256)
    tiles = share // tile
    at = (lax.axis_index("dp") * tiles).astype(jnp.int32).reshape(1)
    weight_grads = pl.pallas_call(
        keep_kernel,
        grid_spec=pltpu.PrefetchScalarGridSpec(
            num_scalar_prefetch=1,
            grid=(tiles,),
            in_specs=[
                pl.BlockSpec((tile, hidden), lambda i, at: (i, 0)),
                pl.BlockSpec((tile, hidden), lambda i, at: (at[0] + i, 0)),
                pl.BlockSpec((tile, blocks), lambda i, at: (at[0] + i, 0)),
            ],
            out_specs=pl.BlockSpec((tile, hidden), lambda i, at: (i, 0)),
        ),
        out_shape=jax.ShapeDtypeStruct((share, hidden), f32),
        compiler_params=params(),
        name="keep",
    )(at, summed, w_latent[0], block_exponents[0])
    return (input_grads, weight_grads[None])


def solution(mesh):
    placed = (
        P(("dp", "expert"), None),
        P(("dp", "expert"), None),
        P(("dp", "expert"), None),
        P(("dp", "expert"), None, None),
        P("expert", None, None),
        P("expert", None, None),
    )
    dp = mesh.shape["dp"]

    def body(out_grads, *rest):
        share = out_grads.shape[1] // dp
        plan = local_shares if dp == 2 and share % SHARE_TILE == 0 else local
        return plan(out_grads, *rest)

    return jax.shard_map(
        body,
        mesh=mesh,
        in_specs=placed,
        out_specs=(P(("dp", "expert"), None, None), P("expert", "dp", None)),
        check_vma=False,
    )
```
